128 devices in a mesh: seq: 64 (over z, y, x_hi, core), chan: 2 (over x_lo).
Axes of the slice: x: 4 (x_hi: 2, x_lo: 2; x = x_hi * 2 + x_lo), y: 4, z: 4, core: 2. Of those that a mesh axis runs over, the one named last changes fastest.
Arguments:
- tokens: bfloat16 [16, 4096, 1024], P(None, 'seq', 'chan'), may hold values from -6 to 6
- segments: int32 [16, 4096], P(None, 'seq'), may hold values from 0 to 20, as said below
- w_in: bfloat16 [1024, 3, 1024], P(None, None, 'chan'), may hold values from -0.1875 to 0.1875
- conv_w: bfloat16 [3, 1024], P(None, 'chan'), may hold values from -3 to 3
- w_out: bfloat16 [1024, 1024], P('chan'), may hold values from -0.1875 to 0.1875
- gain_one: bfloat16 [1024], P('chan'), may hold values from 0.25 to 1.75
- gain_two: bfloat16 [1024], P('chan'), may hold values from 0.25 to 1.75
- w_gu: bfloat16 [1024, 2, 4608], P(None, None, 'chan'), may hold values from -0.1875 to 0.1875
- w_down: bfloat16 [4608, 1024], P('chan'), may hold values from -0.125 to 0.125
- cotangent: bfloat16 [16, 4096, 1024], P(None, 'seq', 'chan'), may hold values from -6 to 6
Outputs:
- block_out: bfloat16 [16, 4096, 1024], P(None, 'seq', 'chan')
- d_tokens: float32 [16, 4096, 1024], P(None, 'seq', 'chan')
- grad_in: float32 [1024, 3, 1024], P(None, None, 'chan')
- grad_conv: float32 [3, 1024], P(None, 'chan')
- grad_out: float32 [1024, 1024], P('chan')
- grad_gain_one: float32 [1024], P('chan')
- grad_gain_two: float32 [1024], P('chan')
- grad_gu: float32 [1024, 2, 4608], P(None, None, 'chan')
- grad_down: float32 [4608, 1024], P('chan')
The draws below stay inside these ranges and needn't reach their ends.
Inputs may be any that keep to these rules, and one draw needn't show every extreme that they name: `segments`: within each sequence the numbers start at 0 and rise by one at each new document; every document except a sequence's last has 200 to 2000 tokens; one sequence, drawn from the seed, is a single document, and another is made of documents of exactly 200 tokens but its last.
All inputs are finite; a program needn't handle non-finite values.
Results may differ from the reference program's by a relative error of at most 0.0097.
Values may be sent and summed in bfloat16 or wider, within the bound.
No kernel may reach another device: no remote copies, remote signals or barrier semaphores. Data moves between devices by JAX's collectives and lax.ppermute only.
A program may use at most 256 MiB of HBM per device.

```python
import jax
import jax.numpy as jnp
from jax import lax

D = 1024
FF = 4608
SEQS = 16
DOC_MIN = 200
DOC_MAX = 2000
LEN = 4096


def draw_segments(key, part):
    key = jax.random.fold_in(key, 7)
    key_lengths, key_whole, key_short = jax.random.split(key, 3)
    count = LEN // DOC_MIN + 1
    lengths = jax.random.randint(key_lengths, (SEQS, count), DOC_MIN, DOC_MAX + 1)
    ends = jnp.cumsum(lengths, axis=1)
    positions = jnp.arange(LEN, dtype=jnp.int32)
    numbers = jnp.sum((ends[:, None, :] <= positions[None, :, None]).astype(jnp.int32), axis=2)
    whole = jax.random.randint(key_whole, (), 0, SEQS)
    offset = jax.random.randint(key_short, (), 1, SEQS)
    shortest = (whole + offset) % SEQS
    rows = jnp.arange(SEQS, dtype=jnp.int32)[:, None]
    tight = jnp.broadcast_to((positions // DOC_MIN)[None, :], (SEQS, LEN))
    numbers = jnp.where(rows == shortest, tight, numbers)
    return jnp.where(rows == whole, 0, numbers).astype(jnp.int32)


def levels(rng, extent, cuts, least, top_value):
    def one(position, blocks):
        draws = jax.random.uniform(jax.random.fold_in(jax.random.fold_in(rng, 6), position), (blocks,), jnp.float32, least / len(cuts), top_value / len(cuts))
        return jnp.repeat(jnp.exp(draws), extent[position] // blocks).reshape((-1,) + (1,) * (len(extent) - position - 1))

    level = one(*cuts[0])
    for cut in cuts[1:]:
        level = level * one(*cut)
    return level


def bell_draw(own_key, shape, deviation, limit, cuts=(), held_as=jnp.bfloat16):
    values = deviation * jax.random.normal(own_key, shape, jnp.float32)
    if cuts:
        values = values * levels(own_key, shape, cuts, -0.22, 0.18)
    return jnp.clip(values, -limit, limit).astype(held_as)


def setup_inputs(seed: int = 0) -> dict:
    key_of = jax.random.split(jax.random.key(seed), 11)
    tokens = bell_draw(key_of[0], (SEQS, LEN, D), 1.0, 6.0, ((1, 64), (2, 2)))
    segments = draw_segments(jax.random.fold_in(key_of[10], 71), 0)
    w_in = bell_draw(key_of[2], (D, 3, D), D ** -0.5, 0.1875, ((2, 2),))
    conv_w = bell_draw(key_of[3], (3, D), 0.6, 3.0, ((1, 2),))
    w_out = bell_draw(key_of[4], (D, D), D ** -0.5, 0.1875, ((0, 2),))
    gain_one = jnp.clip(1.0 + 0.15 * jax.random.normal(key_of[5], (D,), jnp.float32), 0.25, 1.75).astype(jnp.bfloat16)
    gain_two = jnp.clip(1.0 + 0.15 * jax.random.normal(key_of[6], (D,), jnp.float32), 0.25, 1.75).astype(jnp.bfloat16)
    w_gu = bell_draw(key_of[7], (D, 2, FF), D ** -0.5, 0.1875, ((2, 2),))
    w_down = bell_draw(key_of[8], (FF, D), (FF // 2) ** -0.5, 0.125, ((0, 2),))
    cotangent = bell_draw(key_of[9], (SEQS, LEN, D), 1.0, 6.0, ((1, 64), (2, 2)))
    return {"tokens": tokens, "segments": segments, "w_in": w_in, "conv_w": conv_w, "w_out": w_out, "gain_one": gain_one, "gain_two": gain_two, "w_gu": w_gu, "w_down": w_down, "cotangent": cotangent}


@jax.custom_vjp
def low(v):
    return lax.optimization_barrier(v.astype(jnp.bfloat16)).astype(jnp.float32)

@jax.custom_vjp
def low_back(v):
    return v

def low_keep(v):
    return (low(v), None)

def low_pass(kept, grad):
    return (grad,)

def back_keep(v):
    return (v, None)

def back_low(kept, grad):
    return (low(grad),)
low.defvjp(low_keep, low_pass)
low_back.defvjp(back_keep, back_low)
epsilon = 1e-05
highest = lax.Precision.HIGHEST

def matmul(left, right):
    return jnp.dot(left, right, precision=highest, preferred_element_type=jnp.float32)

def rms_scale(stream):
    return lax.rsqrt(lax.optimization_barrier(jnp.mean(stream * stream, axis=-1, keepdims=True)) + epsilon)

def shifted(values, steps):
    return jnp.pad(values, ((steps, 0), (0, 0)))[:values.shape[0]]

def forward(stream, segment, w_in, conv_w, w_out, gain_one, gain_two, w_gu, w_down):
    scale_one = rms_scale(stream)
    normed_one = low(stream * scale_one * gain_one)
    mixed = low_back(matmul(normed_one, w_in.reshape(D, 3 * D))).reshape(-1, 3, D)
    gated = low(mixed[:, 0] * mixed[:, 2])
    same_one = jnp.concatenate([jnp.zeros((1,), bool), segment[1:] == segment[:-1]]).astype(gated.dtype)
    same_two = jnp.concatenate([jnp.zeros((2,), bool), segment[2:] == segment[:-2]]).astype(gated.dtype)
    conv_out = conv_w[0] * gated + conv_w[1] * same_one[:, None] * shifted(gated, 1)
    conv_out = conv_out + conv_w[2] * same_two[:, None] * shifted(gated, 2)
    branch = low(mixed[:, 1] * conv_out)
    resid = stream + low_back(matmul(branch, w_out))
    scale_two = rms_scale(resid)
    normed_two = low(resid * scale_two * gain_two)
    gate_up = low_back(matmul(normed_two, w_gu.reshape(D, 2 * FF))).reshape(-1, 2, FF)
    hidden = low(jax.nn.silu(gate_up[:, 0]) * gate_up[:, 1])
    return resid + low_back(matmul(hidden, w_down))

def reference(tokens, segments, w_in, conv_w, w_out, gain_one, gain_two, w_gu, w_down, cotangent):
    weights = tuple((array.astype(jnp.float32) for array in (w_in, conv_w, w_out, gain_one, gain_two, w_gu, w_down)))

    def per_sequence(totals, inputs):
        stream, segment, upstream = inputs

        def closed(stream_in, *params):
            return forward(stream_in, segment, *params)
        output, pull = jax.vjp(closed, stream.astype(jnp.float32), *weights)
        grads = pull(upstream.astype(jnp.float32))
        totals = tuple((total + grad for total, grad in zip(totals, grads[1:])))
        return (totals, (output.astype(jnp.bfloat16), grads[0]))
    zeros = tuple((jnp.zeros(weight.shape, jnp.float32) for weight in weights))
    totals, (outputs, input_grad) = lax.scan(per_sequence, zeros, (tokens, segments, cotangent))
    return (outputs, input_grad, totals[0], totals[1], totals[2], totals[3], totals[4], totals[5], totals[6])
```

```python
import jax
import jax.numpy as jnp
from jax import lax
from jax.experimental import pallas as pl
from jax.experimental.pallas import tpu as pltpu
from jax.sharding import PartitionSpec as P

F32 = jnp.float32
BF16 = jnp.bfloat16
D = 1024
HALF = D // 2
TILE = 256
epsilon = 1e-05
EVERYWHERE = ("seq", "chan")
VMEM_LIMIT = 60 << 20


def route(target):
    pairs = []
    for z in range(4):
        for y in range(4):
            for x in range(4):
                for c in range(2):
                    to_z, to_y, to_x, to_c = target(z, y, x, c)
                    here = (((z * 4 + y) * 2 + x // 2) * 2 + c) * 2 + x % 2
                    there = (((to_z * 4 + to_y) * 2 + to_x // 2) * 2 + to_c) * 2 + to_x % 2
                    pairs.append((here, there))
    return pairs


def near(v):
    return v ^ 1


def wrap(v):
    return 3 - v


SWAP_CORE = route(lambda z, y, x, c: (z, y, x, 1 - c))
SWAP_CHAN = route(lambda z, y, x, c: (z, y, x ^ 1, c))
SWAP_FAR = route(lambda z, y, x, c: (z, y, 3 - x, c))
SWAP_K = route(lambda z, y, x, c: (z, y, x ^ 2, c))
SWAP_Z1 = route(lambda z, y, x, c: ((wrap if c else near)(z), y, x, c))
SWAP_Z2 = route(lambda z, y, x, c: ((near if c else wrap)(z), y, x, c))
SWAP_Y1 = route(lambda z, y, x, c: (z, (wrap if c else near)(y), x, c))
SWAP_Y2 = route(lambda z, y, x, c: (z, (near if c else wrap)(y), x, c))


def swap(value, pairs):
    return lax.ppermute(value, EVERYWHERE, pairs)


def from_behind(value, steps):
    count = lax.axis_size("seq")
    leading, last = max(0, -steps), min(count, count - steps)
    return lax.ppermute(value, "seq", [(source, source + steps) for source in range(leading, last)])


def placement():
    s = lax.axis_index("seq")
    c, k, y, z = s & 1, (s >> 1) & 1, (s >> 2) & 3, s >> 4
    inner_z, outer_z = ((z + 1) >> 1) & 1, z >> 1
    inner_y, outer_y = ((y + 1) >> 1) & 1, y >> 1
    z1 = jnp.where(c == 0, inner_z, outer_z)
    z2 = jnp.where(c == 0, outer_z, inner_z)
    y1 = jnp.where(c == 0, inner_y, outer_y)
    y2 = jnp.where(c == 0, outer_y, inner_y)
    return {"c": c, "k": k, "z1": z1, "z2": z2, "y1": y1, "y2": y2}


PAIRS = {"c": SWAP_CORE, "k": SWAP_K, "z1": SWAP_Z1, "z2": SWAP_Z2, "y1": SWAP_Y1, "y2": SWAP_Y2}
ORDER_ONE = ("z1", "z2", "y1", "y2", "k")
ORDER_TWO = ("y1", "y2", "z1", "z2", "k")


def halve(value, bit, step):
    rows = value.shape[0] // 2
    keep = lax.dynamic_slice_in_dim(value, bit * rows, rows, 0)
    send = lax.dynamic_slice_in_dim(value, (1 - bit) * rows, rows, 0)
    got = swap(send, PAIRS[step])
    return (keep.astype(F32) + got.astype(F32)).astype(BF16)


def double(value, bit, step):
    got = swap(value, PAIRS[step])
    return jnp.where(bit == 0, jnp.concatenate([value, got]), jnp.concatenate([got, value]))


def scatter_sum(value, at, order):
    for step in order:
        value = halve(value, at[step], step)
    return value


def gather(value, at, order):
    for step in reversed(order):
        value = double(value, at[step], step)
    return value


def contract(left, right, over_left, over_right):
    return lax.dot_general(
        left, right, (((over_left,), (over_right,)), ((), ())), preferred_element_type=F32
    )


def feed_forward_kernel(normed, cot, w_gate, w_up, w_down, grads, ffn, d_normed):
    @pl.when(pl.program_id(0) == 0)
    def _():
        ffn[...] = jnp.zeros_like(ffn)
        d_normed[...] = jnp.zeros_like(d_normed)

    w_gu = jnp.concatenate([w_gate[...], w_up[...]], axis=1)
    gate_up = contract(normed[...], w_gu, 1, 0)
    gate, up = gate_up[:, :TILE], gate_up[:, TILE:]
    sigma = jax.nn.sigmoid(gate)
    silu_gate = gate * sigma
    hidden = (silu_gate * up).astype(BF16)
    ffn[...] += contract(hidden, w_down[...], 1, 0)
    d_hidden = contract(cot[...], w_down[...], 1, 1)
    d_gate = (d_hidden * up * sigma * (1.0 + gate * (1.0 - sigma))).astype(BF16)
    d_up = (d_hidden * silu_gate).astype(BF16)
    d_gate_up = jnp.concatenate([d_gate, d_up], axis=1)
    grads[:D, :] = contract(normed[...], d_gate_up, 0, 0).astype(BF16)
    grad_down = contract(hidden, cot[...], 0, 0).astype(BF16)
    grads[D : D + TILE, :] = grad_down[:, :HALF]
    grads[D + TILE :, :] = grad_down[:, HALF:]
    d_normed[...] += contract(d_gate_up, w_gu, 1, 1)


def feed_forward(normed, cot, w_gate, w_up, w_down):
    rows, units = normed.shape[0], w_down.shape[0]
    whole = lambda j: (0, 0)
    return pl.pallas_call(
        feed_forward_kernel,
        grid=(units // TILE,),
        in_specs=[
            pl.BlockSpec((rows, D), whole),
            pl.BlockSpec((rows, D), whole),
            pl.BlockSpec((D, TILE), lambda j: (0, j)),
            pl.BlockSpec((D, TILE), lambda j: (0, j)),
            pl.BlockSpec((TILE, D), lambda j: (j, 0)),
        ],
        out_specs=[
            pl.BlockSpec((D + 2 * TILE, 2 * TILE), lambda j: (0, j)),
            pl.BlockSpec((rows, D), whole),
            pl.BlockSpec((rows, D), whole),
        ],
        out_shape=[
            jax.ShapeDtypeStruct((D + 2 * TILE, 2 * units), BF16),
            jax.ShapeDtypeStruct((rows, D), F32),
            jax.ShapeDtypeStruct((rows, D), F32),
        ],
        compiler_params=pltpu.CompilerParams(vmem_limit_bytes=VMEM_LIMIT),
    )(normed, cot, w_gate, w_up, w_down)


def unlay_kernel(packed, out_ref):
    for j in range(out_ref.shape[2] // TILE):
        for k in range(2):
            at = (2 * j + k) * TILE
            out_ref[:, k, j * TILE : (j + 1) * TILE] = packed[:, at : at + TILE].astype(F32)


def unlay_gate_up(packed):
    units = packed.shape[1] // 2
    rows = 128
    return pl.pallas_call(
        unlay_kernel,
        grid=(D // rows,),
        in_specs=[pl.BlockSpec((rows, 2 * units), lambda i: (i, 0))],
        out_specs=pl.BlockSpec((rows, 2, units), lambda i: (i, 0, 0)),
        out_shape=jax.ShapeDtypeStruct((D, 2, units), F32),
        compiler_params=pltpu.CompilerParams(vmem_limit_bytes=VMEM_LIMIT),
    )(packed)


def unlay_down(packed):
    units = packed.shape[1] // 2
    tiles = units // TILE
    blocks = packed.reshape(2, TILE, tiles, HALF).transpose(2, 1, 0, 3)
    return blocks.reshape(units, D).astype(F32)


def partner_weights(w_in, w_out, at):
    parts = []
    for which, order in enumerate((("c",) + ORDER_ONE[:4], ("c",) + ORDER_TWO[:4])):
        shard = 0
        for step in order:
            shard = shard * 2 + at[step]
        rows = HALF // 32
        mine = lax.dynamic_slice_in_dim(w_in, which * HALF + shard * rows, rows, 1)
        half = w_out[:, which * HALF : (which + 1) * HALF]
        mine_out = lax.dynamic_slice_in_dim(half, shard * rows, rows, 0)
        packed = jnp.concatenate([mine.reshape(3 * rows, HALF), mine_out], axis=0)
        packed = swap(packed, SWAP_FAR)
        whole = gather(packed, at, order).reshape(32, 4, rows, HALF).transpose(1, 0, 2, 3)
        parts.append(whole.reshape(4, HALF, HALF))
    return (
        jnp.concatenate([parts[0][:3], parts[1][:3]], axis=1),
        jnp.concatenate([parts[0][3], parts[1][3]], axis=1),
    )


def per_device(tokens, segments, w_in, conv_w, w_out, gain_one, gain_two, w_gu, w_down, cotangent):
    seqs, span, _ = tokens.shape
    rows, part = seqs * span, seqs * span // 2
    some = seqs // 2
    a = lax.axis_index("chan")
    at = placement()

    def ordered(own, other):
        return jnp.where(
            a == 0,
            jnp.concatenate([own, other], axis=-1),
            jnp.concatenate([other, own], axis=-1),
        )

    def own_part(value):
        return lax.dynamic_slice_in_dim(value, a * part, part, 0)

    def own_half(value):
        return lax.dynamic_slice_in_dim(value, a * HALF, HALF, value.ndim - 1)

    def other_half(value):
        return lax.dynamic_slice_in_dim(value, (1 - a) * HALF, HALF, value.ndim - 1)

    tokens = tokens.reshape(rows, HALF)
    cotangent = cotangent.reshape(rows, HALF)
    small = jnp.concatenate([conv_w, gain_one[None], gain_two[None]], axis=0)
    other_small = swap(small, SWAP_CHAN)
    other_tokens = swap(tokens, SWAP_CHAN)
    w_in = w_in.transpose(1, 0, 2)
    other_in, other_out = partner_weights(w_in, w_out, at)
    late_cotangent, _ = lax.optimization_barrier((cotangent, other_tokens))
    other_cotangent = swap(late_cotangent, SWAP_CHAN)

    taps = jnp.concatenate([small[:3], other_small[:3]], axis=1).astype(F32)
    gains = ordered(small[3:], other_small[3:]).astype(F32)
    gain_first, gain_second = gains[0], gains[1]
    w_gate, w_up = w_gu[:, 0], w_gu[:, 1]

    stream = ordered(tokens, other_tokens).astype(F32)
    scale_one = lax.rsqrt(jnp.mean(stream * stream, axis=-1, keepdims=True) + epsilon)
    normed_one = (stream * scale_one * gain_first).astype(BF16)

    def mix(k):
        return jnp.concatenate(
            [contract(normed_one, w_in[k], 1, 0), contract(normed_one, other_in[k], 1, 0)], axis=1
        )

    mixed_b, mixed_c, mixed_x = mix(0), mix(1), mix(2)
    gated = (mixed_b * mixed_x).astype(BF16).reshape(seqs, span, D)
    earlier = from_behind(gated[:, -2:], 1)
    earlier_ids = from_behind(segments[:, -2:].astype(BF16), 1)
    ext_gated = jnp.concatenate([earlier, gated], axis=1)
    ext_ids = jnp.concatenate([earlier_ids.astype(F32), segments.astype(F32)], axis=1)
    same_one = (ext_ids[:, 2:] == ext_ids[:, 1:-1]).astype(F32)[..., None]
    same_two = (ext_ids[:, 2:] == ext_ids[:, :-2]).astype(F32)[..., None]
    gated_now = ext_gated[:, 2:].astype(F32)
    gated_one = ext_gated[:, 1:-1].astype(F32) * same_one
    gated_two = ext_gated[:, :-2].astype(F32) * same_two
    conv_out = (taps[0] * gated_now + taps[1] * gated_one + taps[2] * gated_two).reshape(rows, D)
    branch = (mixed_c * conv_out).astype(BF16)
    resid = (
        stream
        + contract(branch[:, :HALF], w_out, 1, 0)
        + contract(branch[:, HALF:], other_out, 1, 0)
    )
    scale_two = lax.rsqrt(jnp.mean(resid * resid, axis=-1, keepdims=True) + epsilon)
    normed_two = (resid * scale_two * gain_second).astype(BF16)

    cot = ordered(cotangent, other_cotangent)
    grads, ffn, d_normed_two = feed_forward(normed_two, cot, w_gate, w_up, w_down)

    sent_back = lax.dynamic_slice_in_dim(d_normed_two, (1 - a) * part, part, 0).astype(BF16)
    d_normed_two = own_part(d_normed_two) + swap(sent_back, SWAP_CHAN).astype(F32)

    wide = grads.shape[1] // 2
    shared = halve(grads, at["c"], "c")
    one = scatter_sum(shared[:, :wide], at, ORDER_ONE)
    two = scatter_sum(shared[:, wide:], at, ORDER_TWO)

    block_out = own_half(resid) + own_half(ffn) + swap(
        other_half(ffn).astype(BF16), SWAP_CHAN
    ).astype(F32)
    block_out = block_out.astype(BF16)

    resid, scale_two, stream, scale_one = (
        own_part(resid), own_part(scale_two), own_part(stream), own_part(scale_one)
    )
    pulled = d_normed_two * gain_second
    inner = jnp.sum(pulled * resid, axis=-1, keepdims=True)
    d_resid = (
        own_part(cot).astype(F32)
        + scale_two * pulled
        - resid * (scale_two * scale_two * scale_two * inner / D)
    )
    grad_gain_two = jnp.sum(d_normed_two * resid * scale_two, axis=0)

    d_branch_out = d_resid.astype(BF16)
    d_branch = jnp.concatenate(
        [contract(d_branch_out, w_out, 1, 1), contract(d_branch_out, other_out, 1, 1)], axis=1
    )
    grad_out = contract(own_part(branch), d_branch_out, 0, 0)
    d_c = d_branch * own_part(conv_out)
    d_conv = (d_branch * own_part(mixed_c)).reshape(some, span, D)

    def own_seqs(value):
        return lax.dynamic_slice_in_dim(value, a * some, some, 0)

    same_one, same_two = own_seqs(same_one), own_seqs(same_two)
    grad_conv = [
        jnp.sum(d_conv * own_seqs(value), axis=(0, 1)) for value in (gated_now, gated_one, gated_two)
    ]
    term_one = taps[1] * same_one * d_conv
    term_two = taps[2] * same_two * d_conv
    first = jnp.stack([term_two[:, 0], term_one[:, 0] + term_two[:, 1]], axis=1)
    later = from_behind(first.astype(BF16), -1).astype(F32)
    d_gated = (
        taps[0] * d_conv
        + jnp.pad(term_one[:, 1:], ((0, 0), (0, 1), (0, 0)))
        + jnp.pad(term_two[:, 2:], ((0, 0), (0, 2), (0, 0)))
        + jnp.pad(later, ((0, 0), (span - 2, 0), (0, 0)))
    ).reshape(part, D)
    d_b = (d_gated * own_part(mixed_x)).astype(BF16)
    d_x = (d_gated * own_part(mixed_b)).astype(BF16)
    d_c = d_c.astype(BF16)
    normed_part = own_part(normed_one)
    grad_in = [contract(normed_part, value, 0, 0).astype(BF16) for value in (d_b, d_c, d_x)]
    d_normed_one = sum(
        contract(value[:, :HALF], w_in[k], 1, 1) + contract(value[:, HALF:], other_in[k], 1, 1)
        for k, value in enumerate((d_b, d_c, d_x))
    )
    grad_out = grad_out.astype(BF16)
    grad_out = jnp.concatenate(
        [
            jnp.concatenate([grad_out[:HALF, :HALF], grad_out[HALF:, :HALF]], axis=1),
            jnp.concatenate([grad_out[:HALF, HALF:], grad_out[HALF:, HALF:]], axis=1),
        ],
        axis=0,
    )
    conv_grads = halve(jnp.concatenate(grad_in + [grad_out], axis=0), at["c"], "c")
    deep = conv_grads.shape[0] // 2
    conv_parts = []
    for value, order in ((conv_grads[:deep], ORDER_ONE), (conv_grads[deep:], ORDER_TWO)):
        value = scatter_sum(value, at, order).astype(F32)
        value = (value[:, :HALF] + swap(value[:, HALF:].astype(BF16), SWAP_CHAN).astype(F32)).astype(BF16)
        conv_parts.append(gather(value, at, order))
    conv_grads = double(jnp.concatenate(conv_parts, axis=0), at["c"], "c")

    pulled = d_normed_one * gain_first
    inner = jnp.sum(pulled * stream, axis=-1, keepdims=True)
    d_tokens = d_resid + scale_one * pulled - stream * (
        scale_one * scale_one * scale_one * inner / D
    )
    grad_gain_one = jnp.sum(d_normed_one * stream * scale_one, axis=0)
    got = swap(other_half(d_tokens).astype(BF16), SWAP_CHAN).astype(F32)
    kept = own_half(d_tokens)
    d_tokens = jnp.where(
        a == 0, jnp.concatenate([kept, got], axis=0), jnp.concatenate([got, kept], axis=0)
    )

    gain_grads = jnp.stack([grad_gain_one, grad_gain_two], axis=0)
    own_small = jnp.concatenate(
        [jnp.stack([value[:HALF] for value in grad_conv]), own_half(gain_grads)], axis=0
    )
    other_grads = jnp.concatenate(
        [jnp.stack([value[HALF:] for value in grad_conv]), other_half(gain_grads)], axis=0
    )
    totals = own_small + swap(other_grads, SWAP_CHAN)
    for step in ("c",) + ORDER_ONE:
        totals = totals + swap(totals, PAIRS[step])

    shared = jnp.concatenate([gather(one, at, ORDER_ONE), gather(two, at, ORDER_TWO)], axis=1)
    grads = double(shared, at["c"], "c")
    return (
        block_out.reshape(seqs, span, HALF),
        d_tokens.reshape(seqs, span, HALF),
        conv_grads[: 3 * D].astype(F32).reshape(3, D, HALF).transpose(1, 0, 2),
        totals[:3],
        jnp.concatenate([conv_grads[3 * D : 3 * D + HALF], conv_grads[3 * D + HALF :]], axis=1).astype(F32),
        totals[3],
        totals[4],
        unlay_gate_up(grads[:D]),
        unlay_down(grads[D:]),
    )


def solution(mesh):
    placed = (
        P(None, "seq", "chan"),
        P(None, "seq"),
        P(None, None, "chan"),
        P(None, "chan"),
        P("chan", None),
        P("chan"),
        P("chan"),
        P(None, None, "chan"),
        P("chan", None),
        P(None, "seq", "chan"),
    )
    return jax.shard_map(
        per_device,
        mesh=mesh,
        in_specs=placed,
        out_specs=(
            P(None, "seq", "chan"),
            P(None, "seq", "chan"),
            P(None, None, "chan"),
            P(None, "chan"),
            P("chan", None),
            P("chan"),
            P("chan"),
            P(None, None, "chan"),
            P("chan", None),
        ),
        check_vma=False,
    )
```
